128 devices in a mesh: seq: 16 (over y, z_hi, core), res: 8 (over z_lo, x).
Axes of the slice: x: 4, y: 4, z: 4 (z_hi: 2, z_lo: 2; z = z_hi * 2 + z_lo), core: 2. Of those that a mesh axis runs over, the one named last changes fastest.
Arguments:
- homolog_embedding: bfloat16 [128, 2048, 256], P('seq', 'res'), may hold values from -6 to 6
- pair_features: bfloat16 [2048, 2048, 128], P('res', 'seq'), may hold values from -6 to 6
- sequence_key_mask: int32 [128], replicated, may hold values 0 or 1
- residue_key_mask: int32 [2048], replicated, may hold values 0 or 1
- pair_head_bias_matrix: bfloat16 [128, 8], replicated
- horizontal_probe_weights: bfloat16 [256, 256], replicated, may hold values from -0.375 to 0.375
- horizontal_lookup_weights: bfloat16 [256, 512], replicated, may hold values from -0.375 to 0.375
- horizontal_sigmoid_weights: bfloat16 [256, 256], replicated, may hold values from -0.375 to 0.375
- horizontal_merge_weights: bfloat16 [256, 256], replicated, may hold values from -1.5 to 1.5
- column_query_matrix: bfloat16 [256, 256], replicated
- vertical_lookup_weights: bfloat16 [256, 512], replicated, may hold values from -0.375 to 0.375
- vertical_sigmoid_weights: bfloat16 [256, 256], replicated, may hold values from -0.375 to 0.375
- vertical_merge_weights: bfloat16 [256, 256], replicated, may hold values from -1.5 to 1.5
Outputs:
- alignment_after_rows: bfloat16 [128, 2048, 256], P('seq', 'res')
- alignment_final_state: bfloat16 [128, 2048, 256], P('seq', 'res')
The draws below stay inside these ranges and needn't reach their ends.
All inputs are finite; a program needn't handle non-finite values.
Results may differ from the reference program's by a relative error of at most 0.03.
Values may be sent and summed in bfloat16 or wider, within the bound.
No kernel may reach another device: no remote copies, remote signals or barrier semaphores. Data moves between devices by JAX's collectives and lax.ppermute only.
A program may use at most 128 MiB of HBM per device.

```python
import math
import jax
import jax.numpy as jnp
from jax import lax

EMBED_DIMENSION = 256
HEADCOUNT_PER = 8
CZ = 128
HOMOLOG_NUMBER = 128
PROTEIN_LENGTH = 2048


def draw_pair_head_bias_matrix(key, part):
    key = jax.random.fold_in(key, 11)
    leading_element = jax.random.fold_in(key, 0)
    starting_point = jax.random.normal(leading_element, (CZ, HEADCOUNT_PER), jnp.float32)
    return (starting_point / math.sqrt(CZ)).astype(jnp.bfloat16)


def draw_column_query_matrix(key, part):
    key = jax.random.fold_in(key, 23)
    leading_element = jax.random.fold_in(key, 0)
    starting_point = jax.random.normal(leading_element, (EMBED_DIMENSION, EMBED_DIMENSION), jnp.float32)
    multipliers = jnp.ones((1, HEADCOUNT_PER), jnp.float32)
    multipliers = jnp.repeat(multipliers, EMBED_DIMENSION // HEADCOUNT_PER, axis=1)
    return (starting_point * multipliers / math.sqrt(EMBED_DIMENSION)).astype(jnp.bfloat16)


def with_ends(array, key, least, high):
    dims = array.shape
    index_at = [jax.random.randint(jax.random.fold_in(key, axis), (), 0, dims[axis]) for axis in range(len(dims))]
    array = array.at[tuple(index_at)].set(least)
    longest = dims.index(max(dims))
    index_at[longest] = (index_at[longest] + 1) % dims[longest]
    return array.at[tuple(index_at)].set(high)


def block_scale(stream_key, dims, pieces, low, largest):
    def one(axis_at, shards_of):
        heights = jax.random.uniform(jax.random.fold_in(jax.random.fold_in(stream_key, 6), axis_at), (shards_of,), jnp.float32, low / len(pieces), largest / len(pieces))
        return jnp.repeat(jnp.exp(heights), dims[axis_at] // shards_of).reshape((-1,) + (1,) * (len(dims) - axis_at - 1))

    level = one(*pieces[0])
    for cut in pieces[1:]:
        level = level * one(*cut)
    return level


def noise(key, shape, scale, bound, pieces=(), kind=jnp.bfloat16):
    level = block_scale(key, shape, pieces, -0.22, 0.18) if pieces else 1.0
    entries = jax.random.normal(key, shape, jnp.float32) * scale * level
    return jnp.minimum(jnp.maximum(entries, -bound), bound).astype(kind)


def setup_inputs(seed: int = 0) -> dict:
    splits = jax.random.split(jax.random.key(seed), 14)
    homolog_embedding = noise(splits[0], (HOMOLOG_NUMBER, PROTEIN_LENGTH, EMBED_DIMENSION), 1.0, 6.0, ((0, 16), (1, 8)))
    pair_features = noise(splits[1], (PROTEIN_LENGTH, PROTEIN_LENGTH, CZ), 1.0, 6.0, ((0, 8), (1, 16)))
    sequence_key_mask = with_ends((jax.random.randint(splits[2], (HOMOLOG_NUMBER,), 0, 8) < 7).astype(jnp.int32), jax.random.fold_in(splits[2], 1), 0, 1)
    residue_key_mask = with_ends((jax.random.randint(splits[3], (PROTEIN_LENGTH,), 0, 8) < 7).astype(jnp.int32), jax.random.fold_in(splits[3], 1), 0, 1)
    pair_head_bias_matrix = draw_pair_head_bias_matrix(jax.random.fold_in(splits[13], 71), 0)
    horizontal_probe_weights = noise(splits[5], (EMBED_DIMENSION, EMBED_DIMENSION), EMBED_DIMENSION ** -0.5, 0.375)
    horizontal_lookup_weights = noise(splits[6], (EMBED_DIMENSION, 2 * EMBED_DIMENSION), EMBED_DIMENSION ** -0.5, 0.375)
    horizontal_sigmoid_weights = noise(splits[7], (EMBED_DIMENSION, EMBED_DIMENSION), EMBED_DIMENSION ** -0.5, 0.375)
    horizontal_merge_weights = noise(splits[8], (EMBED_DIMENSION, EMBED_DIMENSION), (EMBED_DIMENSION // 16) ** -0.5, 1.5)
    column_query_matrix = draw_column_query_matrix(jax.random.fold_in(splits[13], 71), 0)
    vertical_lookup_weights = noise(splits[10], (EMBED_DIMENSION, 2 * EMBED_DIMENSION), EMBED_DIMENSION ** -0.5, 0.375)
    vertical_sigmoid_weights = noise(splits[11], (EMBED_DIMENSION, EMBED_DIMENSION), EMBED_DIMENSION ** -0.5, 0.375)
    vertical_merge_weights = noise(splits[12], (EMBED_DIMENSION, EMBED_DIMENSION), (EMBED_DIMENSION // 16) ** -0.5, 1.5)
    return dict(homolog_embedding=homolog_embedding, pair_features=pair_features, sequence_key_mask=sequence_key_mask, residue_key_mask=residue_key_mask, pair_head_bias_matrix=pair_head_bias_matrix, horizontal_probe_weights=horizontal_probe_weights, horizontal_lookup_weights=horizontal_lookup_weights, horizontal_sigmoid_weights=horizontal_sigmoid_weights, horizontal_merge_weights=horizontal_merge_weights, column_query_matrix=column_query_matrix, vertical_lookup_weights=vertical_lookup_weights, vertical_sigmoid_weights=vertical_sigmoid_weights, vertical_merge_weights=vertical_merge_weights)


def layer_normalize(values):
    values = values.astype(jnp.float32)
    center = values - lax.optimization_barrier(jnp.mean(values, axis=-1, keepdims=True))
    spread = lax.optimization_barrier(jnp.mean(center * center, axis=-1, keepdims=True))
    return center * lax.rsqrt(spread + 1e-05)

def attend(normalized_input, residual, query_w, keyval_w, gate_w, out_w, extra, key_mask):
    length, channel_width = normalized_input.shape
    head_size = channel_width // HEADCOUNT_PER
    query_vectors = (jnp.dot(normalized_input, query_w, preferred_element_type=jnp.float32) * (1.0 / math.sqrt(head_size))).astype(jnp.bfloat16)
    query_vectors = query_vectors.reshape(length, HEADCOUNT_PER, head_size)
    key_value_pairs = jnp.dot(normalized_input, keyval_w, preferred_element_type=jnp.float32).astype(jnp.bfloat16)
    keys = key_value_pairs[:, :channel_width].reshape(length, HEADCOUNT_PER, head_size)
    values_part = key_value_pairs[:, channel_width:].reshape(length, HEADCOUNT_PER, head_size)
    scores = jnp.einsum('ihd,jhd->hij', query_vectors.astype(jnp.float32), keys.astype(jnp.float32)) + extra.astype(jnp.float32)
    scores = jnp.where(key_mask[None, None, :] > 0, scores, -1000000000.0)
    weights = jax.nn.softmax(scores, axis=-1).astype(jnp.bfloat16)
    mixed = jnp.einsum('hij,jhd->ihd', weights.astype(jnp.float32), values_part.astype(jnp.float32)).reshape(length, channel_width)
    gate_activation = jax.nn.sigmoid(jnp.dot(normalized_input, gate_w, preferred_element_type=jnp.float32))
    gated = (mixed * gate_activation).astype(jnp.bfloat16)
    update = jnp.dot(gated, out_w, preferred_element_type=jnp.float32)
    return (residual.astype(jnp.float32) + update).astype(jnp.bfloat16)

def reference(homolog_embedding, pair_features, sequence_key_mask, residue_key_mask, pair_head_bias_matrix, horizontal_probe_weights, horizontal_lookup_weights, horizontal_sigmoid_weights, horizontal_merge_weights, column_query_matrix, vertical_lookup_weights, vertical_sigmoid_weights, vertical_merge_weights):

    def bias_row(pair_line):
        normed_line = layer_normalize(pair_line).astype(jnp.bfloat16)
        return jnp.dot(normed_line, pair_head_bias_matrix, preferred_element_type=jnp.float32).astype(jnp.bfloat16)
    bias_rows = lax.map(bias_row, pair_features)
    pair_bias = jnp.transpose(bias_rows, (2, 0, 1))

    def row_single_pass(sequence):
        normalized_input = layer_normalize(sequence).astype(jnp.bfloat16)
        return attend(normalized_input, sequence, horizontal_probe_weights, horizontal_lookup_weights, horizontal_sigmoid_weights, horizontal_merge_weights, pair_bias, residue_key_mask)
    alignment_after_rows = lax.map(row_single_pass, homolog_embedding)
    column_inputs = jnp.transpose(alignment_after_rows, (1, 0, 2))

    def column_single_pass(column):
        normalized_input = layer_normalize(column).astype(jnp.bfloat16)
        return attend(normalized_input, column, column_query_matrix, vertical_lookup_weights, vertical_sigmoid_weights, vertical_merge_weights, jnp.zeros((), jnp.float32), sequence_key_mask)
    alignment_final_state = jnp.transpose(lax.map(column_single_pass, column_inputs), (1, 0, 2))
    return (alignment_after_rows, alignment_final_state)
```

```python
import functools
import math

import jax
import jax.numpy as jnp
from jax import lax
from jax.experimental import pallas as pl
from jax.experimental.pallas import tpu as pltpu
from jax.sharding import PartitionSpec as P

HEADS = 8
LOG2E = math.log2(math.e)
MASKED = -1000000000.0
SAFE_SCORE = 100.0
BF16 = jnp.bfloat16
F32 = jnp.float32
NT = (((1,), (1,)), ((), ()))
VMEM_LIMIT = 60 * 2**20


def whole(*shape):
    return pl.BlockSpec(shape, lambda *_: (0,) * len(shape), pipeline_mode=pl.Buffered(1))


def layer_norm(x):
    center = x - jnp.mean(x, axis=-1, keepdims=True)
    spread = jnp.mean(center * center, axis=-1, keepdims=True)
    return center * lax.rsqrt(spread + 1e-05)


def norm_kernel(x_ref, out_ref):
    out_ref[...] = layer_norm(x_ref[...].astype(F32)).astype(BF16)


def norm_rows(x):
    seqs, res, width = x.shape
    return pl.pallas_call(
        norm_kernel,
        grid=(seqs // 2,),
        name="norm_rows",
        in_specs=[pl.BlockSpec((2, res, width), lambda s: (s, 0, 0))],
        out_specs=pl.BlockSpec((2, res, width), lambda s: (s, 0, 0)),
        out_shape=jax.ShapeDtypeStruct(x.shape, BF16),
    )(x)


def pair_kernel(x_ref, w_ref, out_ref, acc):
    rows, keys, width = x_ref.shape
    x = x_ref[...].reshape(rows * keys, width)
    average = jnp.full((width, width), 1.0 / width, BF16)
    center = x.astype(F32) - jnp.dot(x, average, preferred_element_type=F32)
    square = (center * center).astype(BF16)
    spread = jnp.dot(square, average, preferred_element_type=F32)
    normed = (center * lax.rsqrt(spread + 1e-05)).astype(BF16)
    for i in range(rows):
        acc[i] = lax.dot_general(
            w_ref[...], normed[i * keys : (i + 1) * keys], NT, preferred_element_type=F32
        )
    for h in range(HEADS):
        out_ref[h] = (acc[:, h, :] * LOG2E).astype(BF16)


def pair_bias(pair, head_w):
    rows, keys, width = pair.shape
    step = 32
    return pl.pallas_call(
        pair_kernel,
        grid=(rows // step,),
        name="pair_bias",
        in_specs=[
            pl.BlockSpec((step, keys, width), lambda i: (i, 0, 0)),
            whole(HEADS, width),
        ],
        out_specs=pl.BlockSpec((HEADS, step, keys), lambda i: (0, i, 0)),
        out_shape=jax.ShapeDtypeStruct((HEADS, rows, keys), BF16),
        scratch_shapes=[pltpu.VMEM((step, HEADS, keys), F32)],
        compiler_params=pltpu.CompilerParams(vmem_limit_bytes=VMEM_LIMIT),
    )(pair, head_w.T)


def head_lanes(rows, h, o):
    lane = lax.broadcasted_iota(jnp.int32, (rows, 128), 1) // 32
    return jnp.where(lane == h % 4, o, 0.0)


def row_kernel(
    normed_ref, own_ref, emb_ref, bias_ref, mask_col_ref, mask_row_ref, limit_ref,
    wqk_ref, wv_ref, wg_ref, wm_ref, out_ref, send_ref, va, qt, mixed,
):
    blocks, _, rows, width = normed_ref.shape
    length = blocks * rows
    tiles = bias_ref.shape[0]
    tile = length // tiles
    keep = mask_col_ref[...]

    @pl.when(pl.program_id(0) == 0)
    def _():
        for g in range(2):
            va[g, :, 128:] = jnp.broadcast_to(keep, (length, 128)).astype(BF16)

    def keys(k, count):
        return normed_ref[k : k + count, 0].reshape(count * rows, width)

    for k in range(blocks):
        v = jnp.dot(keys(k, 1), wv_ref[...], preferred_element_type=F32)
        v = (v * keep[k * rows : (k + 1) * rows]).astype(BF16)
        va[0, k * rows : (k + 1) * rows, :128] = v[:, :128]
        va[1, k * rows : (k + 1) * rows, :128] = v[:, 128:]
    own = own_ref[0]
    largest = jnp.zeros((rows, 1), F32)
    for h in range(HEADS):
        q = jnp.dot(own, wqk_ref[:, h * width : (h + 1) * width], preferred_element_type=F32)
        largest = jnp.maximum(largest, jnp.sum(q * q, axis=-1, keepdims=True))
        qt[h] = q.astype(BF16)
    largest = jnp.max(largest)

    def put(h, g, u):
        part = u[:, :128] / u[:, 128:]
        return head_lanes(rows, h, part)

    fast = largest < limit_ref[0]

    @pl.when(fast)
    def _():
        step = 1
        for h in range(HEADS):
            u = None
            for k in range(0, blocks, step):
                s = lax.dot_general(qt[h], keys(k, step), NT, preferred_element_type=F32)
                first = k * rows // tile
                b = [bias_ref[first + t, h] for t in range(step * rows // tile)]
                s = s + jnp.concatenate(b, axis=1).astype(F32)
                e = jnp.exp2(s).astype(BF16)
                d = jnp.dot(
                    e, va[h // 4, k * rows : (k + step) * rows], preferred_element_type=F32
                )
                u = d if u is None else u + d
            g = h // 4
            part = put(h, g, u)
            if h % 4 == 0:
                mixed[:, g * 128 : (g + 1) * 128] = part
            else:
                mixed[:, g * 128 : (g + 1) * 128] += part

    @pl.when(jnp.logical_not(fast))
    def _():
        mixed[...] = jnp.zeros_like(mixed)
        for g in range(2):

            def one(i, carry):
                h = g * 4 + i
                s = lax.dot_general(qt[h], keys(0, blocks), NT, preferred_element_type=F32)
                b = [bias_ref[t, h] for t in range(tiles)]
                s = s + jnp.concatenate(b, axis=1).astype(F32)
                s = jnp.where(mask_row_ref[...] > 0, s, MASKED)
                e = jnp.exp2(s - jnp.max(s, axis=-1, keepdims=True)).astype(BF16)
                u = jnp.dot(e, va[g], preferred_element_type=F32)
                mixed[:, g * 128 : (g + 1) * 128] += put(i, g, u)
                return carry

            lax.fori_loop(0, 4, one, 0)

    gate = jax.nn.sigmoid(jnp.dot(own, wg_ref[...], preferred_element_type=F32))
    gated = (mixed[...] * gate).astype(BF16)
    update = jnp.dot(gated, wm_ref[...], preferred_element_type=F32)
    result = (emb_ref[0].astype(F32) + update).astype(BF16)
    out_ref[0] = result
    send_ref[:, 0] = result.reshape(send_ref.shape[0], send_ref.shape[2], width)


def row_attention(normed, own, emb, bias, mask, limit, wqk, wv, wg, wm, groups):
    blocks, seqs, rows, width = normed.shape
    length = blocks * rows
    tiles = bias.shape[0]
    one = pl.BlockSpec((1, rows, width), lambda s: (s, 0, 0))
    part = rows // groups
    return pl.pallas_call(
        row_kernel,
        grid=(seqs,),
        name="row_attention",
        in_specs=[
            pl.BlockSpec((blocks, 1, rows, width), lambda s: (0, s, 0, 0)),
            one,
            one,
            whole(tiles, HEADS, rows, length // tiles),
            whole(length, 1),
            whole(1, length),
            pl.BlockSpec(memory_space=pltpu.SMEM),
            whole(width, HEADS * width),
            whole(width, width),
            whole(width, width),
            whole(width, width),
        ],
        out_specs=[one, pl.BlockSpec((groups, 1, part, width), lambda s: (0, s, 0, 0))],
        out_shape=[
            jax.ShapeDtypeStruct((seqs, rows, width), BF16),
            jax.ShapeDtypeStruct((groups, seqs, part, width), BF16),
        ],
        scratch_shapes=[
            pltpu.VMEM((2, length, 256), BF16),
            pltpu.VMEM((HEADS, rows, width), BF16),
            pltpu.VMEM((rows, width), F32),
        ],
        compiler_params=pltpu.CompilerParams(vmem_limit_bytes=VMEM_LIMIT),
    )(normed, own, emb, bias, mask.reshape(length, 1), mask.reshape(1, length), limit,
      wqk, wv, wg, wm)


def column_kernel(
    x_ref, mask_ref, wqk_ref, wv_ref, wg_ref, wm_ref, out_ref, raw, normed, done
):
    seqs, res, width = x_ref.shape
    x = x_ref[...].astype(F32)
    raw[...] = x
    normed[...] = layer_norm(x)
    ones = jnp.ones((seqs, 128), BF16)
    mask = mask_ref[...] > 0
    for r in range(res):
        n = normed[:, r, :].astype(BF16)
        v = jnp.dot(n, wv_ref[...], preferred_element_type=F32).astype(BF16)
        q = jnp.dot(n, wqk_ref[...], preferred_element_type=F32).astype(BF16)
        halves = []
        for g in range(2):
            qg = jnp.concatenate(
                [q[:, h * width : (h + 1) * width] for h in range(4 * g, 4 * g + 4)], axis=0
            )
            s = lax.dot_general(qg, n, NT, preferred_element_type=F32)
            s = jnp.where(mask, s, MASKED)
            e = jnp.exp2(s - jnp.max(s, axis=-1, keepdims=True)).astype(BF16)
            va = jnp.concatenate([v[:, g * 128 : (g + 1) * 128], ones], axis=1)
            u = jnp.dot(e, va, preferred_element_type=F32)
            o = u[:, :128] / u[:, 128:]
            halves.append(
                sum(head_lanes(seqs, h, o[h * seqs : (h + 1) * seqs]) for h in range(4))
            )
        gate = jax.nn.sigmoid(jnp.dot(n, wg_ref[...], preferred_element_type=F32))
        gated = (jnp.concatenate(halves, axis=1) * gate).astype(BF16)
        update = jnp.dot(gated, wm_ref[...], preferred_element_type=F32)
        done[:, r, :] = raw[:, r, :] + update
    out_ref[...] = done[...].astype(BF16)


def column_attention(x, mask, wqk, wv, wg, wm):
    seqs, res, width = x.shape
    return pl.pallas_call(
        column_kernel,
        name="column_attention",
        out_shape=jax.ShapeDtypeStruct(x.shape, BF16),
        scratch_shapes=[pltpu.VMEM(x.shape, F32)] * 3,
        compiler_params=pltpu.CompilerParams(vmem_limit_bytes=VMEM_LIMIT),
    )(x, mask.reshape(1, seqs), wqk, wv, wg, wm)


def fold_query_key(query_w, key_w):
    width = query_w.shape[0]
    size = width // HEADS
    q = query_w.reshape(width, HEADS, size)
    k = key_w.reshape(width, HEADS, size)
    both = jnp.einsum("chd,ehd->che", q, k, preferred_element_type=F32)
    return (both * (LOG2E / math.sqrt(size))).astype(BF16).reshape(width, HEADS * width)


def per_device(
    homolog_embedding,
    pair_features,
    sequence_key_mask,
    residue_key_mask,
    pair_head_bias_matrix,
    horizontal_probe_weights,
    horizontal_lookup_weights,
    horizontal_sigmoid_weights,
    horizontal_merge_weights,
    column_query_matrix,
    vertical_lookup_weights,
    vertical_sigmoid_weights,
    vertical_merge_weights,
):
    seqs, res, width = homolog_embedding.shape
    groups = lax.axis_size("seq")
    some = jnp.any(residue_key_mask > 0)
    keep = jnp.where(some, (residue_key_mask > 0).astype(F32), 1.0)
    head_w = jnp.where(some, pair_head_bias_matrix, 0).astype(BF16)
    wqk = fold_query_key(horizontal_probe_weights, horizontal_lookup_weights[:, :width])
    wqk = jnp.where(some, wqk, 0).astype(BF16)
    cqk = fold_query_key(column_query_matrix, vertical_lookup_weights[:, :width])
    norms = jnp.sqrt(jnp.sum(jnp.square(head_w.astype(F32)), axis=0))
    bias_bound = 1.02 * LOG2E * math.sqrt(pair_features.shape[-1]) * jnp.max(norms)
    room = jnp.maximum(SAFE_SCORE - bias_bound, 0.0) / (1.02 * math.sqrt(width))
    limit = (room * room).reshape(1)

    own = norm_rows(homolog_embedding)
    normed = lax.all_gather(own, "res")
    bias = lax.all_gather(pair_bias(pair_features, head_w), "seq")
    after_rows, send = row_attention(
        normed,
        own,
        homolog_embedding,
        bias,
        keep,
        limit,
        wqk,
        horizontal_lookup_weights[:, width:],
        horizontal_sigmoid_weights,
        horizontal_merge_weights,
        groups,
    )
    column = lax.all_to_all(send, "seq", 0, 0, tiled=True)
    result = column_attention(
        column.reshape(groups * seqs, res // groups, width),
        sequence_key_mask,
        cqk,
        vertical_lookup_weights[:, width:],
        vertical_sigmoid_weights,
        vertical_merge_weights,
    )
    back = lax.all_to_all(
        result.reshape(groups, seqs, res // groups, width), "seq", 0, 0, tiled=True
    )
    final = jnp.transpose(back, (1, 0, 2, 3)).reshape(seqs, res, width)
    return after_rows, final


def solution(mesh):
    return jax.shard_map(
        per_device,
        mesh=mesh,
        in_specs=(P("seq", "res", None), P("res", "seq", None)) + (P(),) * 11,
        out_specs=(P("seq", "res", None), P("seq", "res", None)),
        check_vma=False,
    )
```

```python
import functools
import math

import jax
import jax.numpy as jnp
from jax import lax
from jax.experimental import pallas as pl
from jax.experimental.pallas import tpu as pltpu
from jax.sharding import PartitionSpec as P

HEADS = 8
GROUP = 4
LOG2E = math.log2(math.e)
MASKED = -1000000000.0
SAFE_SCORE = 100.0
BF16 = jnp.bfloat16
F32 = jnp.float32
NT = (((1,), (1,)), ((), ()))
VMEM_LIMIT = 60 * 2**20


def cost(micros):
    return pl.CostEstimate(flops=int(micros * 1e9), bytes_accessed=0, transcendentals=0)


def whole(*shape):
    return pl.BlockSpec(shape, lambda *_: (0,) * len(shape), pipeline_mode=pl.Buffered(1))


def right_half(w):
    rows, columns = w.shape
    return pl.BlockSpec((rows, columns // 2), lambda *_: (0, 1), pipeline_mode=pl.Buffered(1))


def layer_norm(x):
    center = x - jnp.mean(x, axis=-1, keepdims=True)
    spread = jnp.mean(center * center, axis=-1, keepdims=True)
    return center * lax.rsqrt(spread + 1e-05)


def after(*arrays):
    return list(arrays), [pl.BlockSpec(memory_space=pl.ANY)] * len(arrays)


def norm_kernel(x_ref, *refs):
    out_ref = refs[-1]
    for s in range(out_ref.shape[0]):
        out_ref[s] = layer_norm(x_ref[s].astype(F32)).astype(BF16)


def norm_rows(x, at, count, late=()):
    _, res, width = x.shape
    args, specs = after(*late)
    return pl.pallas_call(
        norm_kernel,
        grid=(1,),
        name="norm_rows",
        in_specs=[pl.BlockSpec((count, res, width), lambda i: (at // count, 0, 0))] + specs,
        out_specs=pl.BlockSpec((count, res, width), lambda i: (0, 0, 0)),
        out_shape=jax.ShapeDtypeStruct((count, res, width), BF16),
        cost_estimate=cost(2),
    )(x, *args)


def pair_kernel(x_ref, w_ref, mask_ref, *rest):
    out_ref, acc = rest[-2:]
    rows, keys, width = x_ref.shape
    half = rows // 2
    wide = 2 * width
    x = jnp.concatenate([x_ref[:half], x_ref[half:]], axis=-1).reshape(half * keys, wide)
    side = lax.broadcasted_iota(jnp.int32, (wide, wide), 0) // width
    same = side == lax.broadcasted_iota(jnp.int32, (wide, wide), 1) // width
    average = jnp.where(same, 1.0 / width, 0.0).astype(BF16)
    center = x.astype(F32) - jnp.dot(x, average, preferred_element_type=F32)
    square = (center * center).astype(BF16)
    center = center.astype(BF16)
    pick = jnp.where(
        lax.broadcasted_iota(jnp.int32, (2 * HEADS, wide), 0) // HEADS
        == lax.broadcasted_iota(jnp.int32, (2 * HEADS, wide), 1) // width,
        1.0 / width,
        0.0,
    ).astype(BF16)
    head_w = w_ref[...].astype(F32).T
    zero = jnp.zeros_like(head_w)
    head_w = jnp.concatenate(
        [
            jnp.concatenate([head_w, zero], axis=1),
            jnp.concatenate([zero, head_w], axis=1),
        ],
        axis=0,
    ).astype(BF16)
    for i in range(0, half, 2):
        here = slice(i * keys, (i + 2) * keys)
        both = lax.dot_general(head_w, center[here], NT, preferred_element_type=F32)
        spread = lax.dot_general(pick, square[here], NT, preferred_element_type=F32)
        both = both * lax.rsqrt(spread + 1e-05)
        for t in range(2):
            acc[i + t] = both[:HEADS, t * keys : (t + 1) * keys]
            acc[half + i + t] = both[HEADS:, t * keys : (t + 1) * keys]
    mask = mask_ref[...]
    here = mask_ref[pl.ds(lax.axis_index("seq"), 1), :]
    none = jnp.max(mask) <= 0
    keep = here > 0
    scale = jnp.where(none, 0.0, LOG2E)
    masked = jnp.where(none, 0.0, MASKED * LOG2E)
    for h in range(HEADS):
        b = jnp.where(keep, acc[:, h, :] * scale, masked)
        out_ref[h] = b.astype(BF16)


def pair_bias(pair, at, rows, head_w, mask, late=()):
    _, keys, width = pair.shape
    step = 64
    args, specs = after(*late)
    return pl.pallas_call(
        pair_kernel,
        grid=(rows // step,),
        name="pair_bias",
        in_specs=[
            pl.BlockSpec((step, keys, width), lambda i: (at // step + i, 0, 0)),
            whole(width, HEADS),
            whole(mask.shape[0] // keys, keys),
        ]
        + specs,
        out_specs=pl.BlockSpec((HEADS, step, keys), lambda i: (0, i, 0)),
        out_shape=jax.ShapeDtypeStruct((HEADS, rows, keys), BF16),
        scratch_shapes=[pltpu.VMEM((step, HEADS, keys), F32)],
        compiler_params=pltpu.CompilerParams(vmem_limit_bytes=VMEM_LIMIT),
        cost_estimate=cost(6),
    )(pair, head_w, mask.reshape(-1, keys), *args)


def head_lanes(rows, h, o):
    lane = lax.broadcasted_iota(jnp.int32, (rows, 128), 1) // 32
    return jnp.where(lane == h % 4, o, 0.0)


def query_kernel(own_ref, wqk_ref, wg_ref, limit_ref, q_ref, gate_ref, fast_ref):
    _, rows, width = own_ref.shape
    own = own_ref[0]
    largest = jnp.zeros((rows, 1), F32)
    for h in range(HEADS):
        q = jnp.dot(own, wqk_ref[:, h * width : (h + 1) * width], preferred_element_type=F32)
        largest = jnp.maximum(largest, jnp.sum(q * q, axis=-1, keepdims=True))
        q_ref[0, h] = q.astype(BF16)
    gate_ref[0] = jax.nn.sigmoid(jnp.dot(own, wg_ref[...], preferred_element_type=F32))
    fast = (jnp.max(largest) < limit_ref[0]).astype(jnp.int32)

    @pl.when(pl.program_id(0) == 0)
    def _():
        fast_ref[0] = 1

    fast_ref[0] = fast_ref[0] * fast


def row_queries(own, wqk, wg, limit):
    seqs, rows, width = own.shape
    smem = pl.BlockSpec(memory_space=pltpu.SMEM)
    return pl.pallas_call(
        query_kernel,
        grid=(seqs,),
        name="row_queries",
        in_specs=[
            pl.BlockSpec((1, rows, width), lambda s: (s, 0, 0)),
            whole(*wqk.shape),
            whole(*wg.shape),
            smem,
        ],
        out_specs=[
            pl.BlockSpec((1, HEADS, rows, width), lambda s: (s, 0, 0, 0)),
            pl.BlockSpec((1, rows, width), lambda s: (s, 0, 0)),
            smem,
        ],
        out_shape=[
            jax.ShapeDtypeStruct((seqs, HEADS, rows, width), BF16),
            jax.ShapeDtypeStruct((seqs, rows, width), F32),
            jax.ShapeDtypeStruct((1,), jnp.int32),
        ],
        cost_estimate=cost(6),
    )(own, wqk, wg, limit)


def value_kernel(*refs):
    n = len(refs) // 2
    for x, out in zip(refs[:n], refs[n + 1 :]):
        out[0] = jnp.dot(x[0], refs[n][...], preferred_element_type=F32).astype(BF16)


def row_values(blocks, wv):
    seqs, rows, width = blocks[0].shape
    one = pl.BlockSpec((1, rows, width), lambda s: (s, 0, 0))
    return pl.pallas_call(
        value_kernel,
        grid=(seqs,),
        name="row_values",
        in_specs=[one] * len(blocks) + [right_half(wv)],
        out_specs=[one] * len(blocks),
        out_shape=[jax.ShapeDtypeStruct(x.shape, BF16) for x in blocks],
        cost_estimate=cost(1.5 * len(blocks)),
    )(*blocks, wv)


def row_kernel(spec, *refs):
    n_skip, turn, offsets, n_values, places = spec
    n_keys = len(offsets)
    refs = list(refs)
    take = lambda n: [refs.pop(0) for _ in range(n)]
    keys, values = take(n_keys), take(n_values)
    bias_in = take(len(places))
    q_ref, gate_ref, emb_ref, fast_ref, wv_ref, wm_ref = take(6)
    take(n_skip)
    out_ref, send_ref, bias, late, sems = refs
    each, block, width = keys[0].shape
    _, heads, rows, tile = bias.shape
    per = block // tile
    pack = max(1, block // rows)
    first = pl.program_id(0) == 0
    seq = lax.axis_index("seq")
    res = lax.axis_index("res")

    def copies():
        here = pl.ds(turn * rows, rows)
        n = 0
        for ref, group in zip(bias_in, places):
            for i, (dy, dz, dc) in enumerate(group):
                place = (
                    lax.rem(seq // 4 + dy, 4) * 4
                    + lax.rem(seq // 2 + dz, 2) * 2
                    + lax.rem(seq + dc, 2)
                )
                yield pltpu.make_async_copy(ref.at[i, :, here], bias.at[place], sems.at[n])
                n += 1

    @pl.when(first)
    def _():
        for c in copies():
            c.start()

    for i in range(each):
        for k in range(n_values, n_keys):
            v = jnp.dot(keys[k][i], wv_ref[...], preferred_element_type=F32)
            late[i, k - n_values] = v.astype(BF16)

    @pl.when(first)
    def _():
        for c in copies():
            c.wait()

    ones = jnp.ones((block, 128), BF16)

    def value(i, g, k):
        lanes = slice(g * 128, (g + 1) * 128)
        v = values[k][i, :, lanes] if k < n_values else late[i, k - n_values, :, lanes]
        return jnp.concatenate([v, ones], axis=1)

    at = [
        (lax.rem(res // 4 + dz, 2) * 4 + lax.rem(res + dx, 4)) * per for dz, dx in offsets
    ]

    def scores(i, h, k):
        q = q_ref[i, h : h + pack].reshape(pack * rows, width)
        s = lax.dot_general(q, keys[k][i], NT, preferred_element_type=F32)
        b = [bias[at[k] + t, h : h + pack].reshape(pack * rows, tile) for t in range(per)]
        return s + jnp.concatenate(b, axis=1).astype(F32)

    def mix(i, with_top):
        halves = []
        for g in range(2):
            total = None
            for h in range(g * GROUP, (g + 1) * GROUP, pack):
                top = None
                if with_top:
                    tops = [
                        jnp.max(scores(i, h, k), axis=-1, keepdims=True) for k in range(n_keys)
                    ]
                    top = functools.reduce(jnp.maximum, tops)
                u = None
                for k in range(n_keys):
                    s = scores(i, h, k)
                    e = jnp.exp2(s - top if with_top else s).astype(BF16)
                    d = jnp.dot(e, value(i, g, k), preferred_element_type=F32)
                    u = d if u is None else u + d
                o = u[:, :128] / u[:, 128:]
                for j in range(pack):
                    part = head_lanes(rows, h + j, o[j * rows : (j + 1) * rows])
                    total = part if total is None else total + part
            halves.append(total)
        gated = (jnp.concatenate(halves, axis=1) * gate_ref[i]).astype(BF16)
        update = jnp.dot(gated, wm_ref[...], preferred_element_type=F32)
        result = (emb_ref[i].astype(F32) + update).astype(BF16)
        out_ref[i] = result
        send_ref[:, i] = result.reshape(send_ref.shape[0], send_ref.shape[2], width)

    fast = fast_ref[0] > 0

    @pl.when(fast)
    def _():
        for i in range(each):
            mix(i, False)

    @pl.when(jnp.logical_not(fast))
    def _():
        lax.fori_loop(0, each, lambda i, carry: (mix(i, True), carry)[1], 0)


def row_attention(keys, values, bias, queries, gate, fast, emb, wv, wm, turn, rows_done=None):
    offsets, places = tuple(keys), tuple(bias)
    seqs, block, width = emb.shape
    _, heads, block, tile = bias[places[0]].shape
    tiles = sum(len(group) for group in places)
    rows = block // 2
    parts = lax.axis_size("seq")
    part = rows // parts
    each = 1
    mine = pl.BlockSpec((each, rows, width), lambda s: (s, turn, 0))
    args = [*keys.values(), *values, *bias.values(), queries, gate, emb, fast, wv, wm]
    specs = [pl.BlockSpec((each, block, width), lambda s: (s, 0, 0))] * (len(keys) + len(values))
    specs += [pl.BlockSpec(memory_space=pl.ANY)] * len(bias)
    specs += [pl.BlockSpec((each, heads, rows, width), lambda s: (s, 0, turn, 0)), mine, mine]
    specs += [pl.BlockSpec(memory_space=pltpu.SMEM), right_half(wv), whole(*wm.shape)]
    aliases = {}
    skipped = []
    if rows_done is not None:
        aliases[len(args)] = 0
        skipped.append(rows_done)
    skip_args, skip_specs = after(*skipped)
    spec = (len(skipped), turn, offsets, len(values), places)
    return pl.pallas_call(
        functools.partial(row_kernel, spec),
        grid=(seqs // each,),
        name="row_attention",
        in_specs=specs + skip_specs,
        out_specs=[mine, pl.BlockSpec((parts, each, part, width), lambda s: (0, s, 0, 0))],
        out_shape=[
            jax.ShapeDtypeStruct(emb.shape, BF16),
            jax.ShapeDtypeStruct((parts, seqs, part, width), BF16),
        ],
        scratch_shapes=[
            pltpu.VMEM((tiles, heads, rows, tile), BF16),
            pltpu.VMEM((each, len(keys) - len(values), block, width), BF16),
            pltpu.SemaphoreType.DMA((tiles,)),
        ],
        input_output_aliases=aliases,
        compiler_params=pltpu.CompilerParams(vmem_limit_bytes=VMEM_LIMIT),
        cost_estimate=cost(22),
    )(*args, *skip_args)


def column_kernel(
    x_ref, mask_ref, wqk_ref, wv_ref, wg_ref, wm_ref, *rest
):
    out_ref, raw, normed, done, qs = rest[-5:]
    groups, each, res, width = x_ref.shape
    seqs = groups * each
    x = x_ref[...].astype(F32)
    raw[...] = x
    normed[...] = layer_norm(x)
    ones = jnp.ones((seqs, 128), BF16)
    mask = mask_ref[...] > 0
    span = range(res)
    n = [normed[:, :, r, :].reshape(seqs, width).astype(BF16) for r in span]
    flat = jnp.concatenate(n, axis=0)
    v = jnp.dot(flat, wv_ref[...], preferred_element_type=F32).astype(BF16)
    gate = jax.nn.sigmoid(jnp.dot(flat, wg_ref[...], preferred_element_type=F32))
    for h in range(HEADS):
        q = jnp.dot(flat, wqk_ref[:, h * width : (h + 1) * width], preferred_element_type=F32)
        q = q.astype(BF16)
        for r in span:
            qs[r, h // 4, (h % 4) * seqs : (h % 4 + 1) * seqs] = q[r * seqs : (r + 1) * seqs]
    mixed = []
    for r in span:
        halves = []
        for g in range(2):
            s = lax.dot_general(qs[r, g], n[r], NT, preferred_element_type=F32)
            s = jnp.where(mask, s, MASKED)
            e = jnp.exp2(s - jnp.max(s, axis=-1, keepdims=True)).astype(BF16)
            va = jnp.concatenate(
                [v[r * seqs : (r + 1) * seqs, g * 128 : (g + 1) * 128], ones], axis=1
            )
            u = jnp.dot(e, va, preferred_element_type=F32)
            o = u[:, :128] / u[:, 128:]
            halves.append(
                sum(head_lanes(seqs, h, o[h * seqs : (h + 1) * seqs]) for h in range(4))
            )
        mixed.append(jnp.concatenate(halves, axis=1))
    gated = (jnp.concatenate(mixed, axis=0) * gate).astype(BF16)
    update = jnp.dot(gated, wm_ref[...], preferred_element_type=F32)
    for r in span:
        before = raw[:, :, r, :]
        done[:, :, r, :] = before + update[r * seqs : (r + 1) * seqs].reshape(before.shape)
    out_ref[...] = done[...].astype(BF16)


def column_attention(x, mask, wqk, wv, wg, wm, late=()):
    args, specs = after(*late)
    return pl.pallas_call(
        column_kernel,
        grid=(1,),
        name="column_attention",
        in_specs=[whole(*x.shape), whole(1, mask.shape[0]), whole(*wqk.shape), right_half(wv)]
        + [whole(*wg.shape), whole(*wm.shape)]
        + specs,
        out_specs=whole(*x.shape),
        out_shape=jax.ShapeDtypeStruct(x.shape, BF16),
        scratch_shapes=[pltpu.VMEM(x.shape, F32)] * 3
        + [pltpu.VMEM((x.shape[2], 2, 4 * x.shape[0] * x.shape[1], x.shape[3]), BF16)],
        compiler_params=pltpu.CompilerParams(vmem_limit_bytes=VMEM_LIMIT),
        cost_estimate=cost(8),
    )(x, mask.reshape(1, -1), wqk, wv, wg, wm, *args)


def fold_kernel(
    mask_ref, head_ref, rq_ref, rkv_ref, cq_ref, ckv_ref, wqk_ref, cqk_ref, limit_ref
):
    width = rq_ref.shape[0]
    size = width // HEADS
    factor = LOG2E / math.sqrt(size)
    some = jnp.max(mask_ref[...]) > 0
    lane = lax.broadcasted_iota(jnp.int32, (width, width), 1) // size
    for q_ref, k_ref, out_ref, scale in (
        (rq_ref, rkv_ref, wqk_ref, jnp.where(some, factor, 0.0)),
        (cq_ref, ckv_ref, cqk_ref, factor),
    ):
        q, k = q_ref[...], k_ref[:, :width]
        for h in range(HEADS):
            one = jnp.where(lane == h, q, jnp.zeros_like(q))
            both = lax.dot_general(one, k, NT, preferred_element_type=F32)
            out_ref[:, h * width : (h + 1) * width] = (both * scale).astype(BF16)
    head = head_ref[...].astype(F32)
    norm = jnp.max(jnp.sqrt(jnp.sum(head * head, axis=0, keepdims=True)))
    room = SAFE_SCORE - 1.02 * LOG2E * math.sqrt(head.shape[0]) * norm
    room = jnp.maximum(room, 0.0) / (1.02 * math.sqrt(width))
    limit_ref[0] = room * room


def fold_weights(mask, head_w, rq, rkv, cq, ckv):
    width = rq.shape[0]
    vmem = pl.BlockSpec(memory_space=pltpu.VMEM)
    return pl.pallas_call(
        fold_kernel,
        name="fold_weights",
        out_specs=[vmem, vmem, pl.BlockSpec(memory_space=pltpu.SMEM)],
        out_shape=[jax.ShapeDtypeStruct((width, HEADS * width), BF16)] * 2
        + [jax.ShapeDtypeStruct((1,), F32)],
        cost_estimate=cost(3),
    )(mask, head_w, rq, rkv, cq, ckv)


def fetch_seq(x, dy, dz, dc):
    pairs = [
        (((y + dy) % 4) * 4 + ((z + dz) % 2) * 2 + (c + dc) % 2, y * 4 + z * 2 + c)
        for y in range(4)
        for z in range(2)
        for c in range(2)
    ]
    return lax.ppermute(x, "seq", pairs)


def fetch_row(x, dz, dx):
    pairs = [
        (((z + dz) % 2) * 4 + (i + dx) % 4, z * 4 + i) for z in range(2) for i in range(4)
    ]
    return lax.ppermute(x, "res", pairs)


def pack_kernel(*refs):
    for i, ref in enumerate(refs[:-1]):
        refs[-1][i] = ref[...]


def pack_blocks(blocks):
    first, *others = blocks[0].shape
    step = first // 4
    return pl.pallas_call(
        pack_kernel,
        grid=(4,),
        name="pack_blocks",
        in_specs=[pl.BlockSpec((step, *others), lambda i: (i, 0, 0))] * len(blocks),
        out_specs=pl.BlockSpec((len(blocks), step, *others), lambda i: (0, i, 0, 0)),
        out_shape=jax.ShapeDtypeStruct((len(blocks), first, *others), blocks[0].dtype),
        cost_estimate=cost(2),
    )(*blocks)


def hold_kernel(*refs):
    pass


def hold(*trees, micros=1):
    boxes = [dict(zip(range(len(t)), t.values())) if isinstance(t, dict) else t for t in trees]
    flat, tree = jax.tree.flatten(boxes)
    any_ = pl.BlockSpec(memory_space=pl.ANY)
    out = pl.pallas_call(
        hold_kernel,
        name="step_done",
        in_specs=[any_] * len(flat),
        out_specs=[any_] * len(flat),
        out_shape=[jax.ShapeDtypeStruct(x.shape, x.dtype) for x in flat],
        input_output_aliases={i: i for i in range(len(flat))},
        cost_estimate=cost(micros),
    )(*flat)
    out = jax.tree.unflatten(tree, out)
    return [dict(zip(t, o.values())) if isinstance(t, dict) else o for t, o in zip(trees, out)]


def per_device(
    homolog_embedding,
    pair_features,
    sequence_key_mask,
    residue_key_mask,
    pair_head_bias_matrix,
    horizontal_probe_weights,
    horizontal_lookup_weights,
    horizontal_sigmoid_weights,
    horizontal_merge_weights,
    column_query_matrix,
    vertical_lookup_weights,
    vertical_sigmoid_weights,
    vertical_merge_weights,
):
    seqs, res, width = homolog_embedding.shape
    groups = lax.axis_size("seq")
    wqk, cqk, limit = fold_weights(
        residue_key_mask.reshape(16, -1),
        pair_head_bias_matrix,
        horizontal_probe_weights,
        horizontal_lookup_weights,
        column_query_matrix,
        vertical_lookup_weights,
    )
    lookup = horizontal_lookup_weights
    a, c = {}, {}
    a[0, 0] = norm_rows(homolog_embedding, 0, seqs)
    a[0, 1] = fetch_row(a[0, 0], 0, 1)
    a[0, 3] = fetch_row(a[0, 0], 0, 3)
    a[1, 0] = fetch_row(a[0, 0], 1, 0)
    c[0, 0] = pair_bias(
        pair_features, 0, res, pair_head_bias_matrix, residue_key_mask, (a[0, 0],)
    )
    c[1, 0] = fetch_seq(c[0, 0], 1, 0, 0)
    c[3, 0] = fetch_seq(c[0, 0], 3, 0, 0)
    bias = {}

    def swap(*offsets):
        both = c[offsets[0]][None] if len(offsets) == 1 else pack_blocks([c[o] for o in offsets])
        bias[tuple((*o, 0) for o in offsets)] = both
        bias[tuple((*o, 1) for o in offsets)] = fetch_seq(both, 0, 0, 1)

    (a,) = hold(a, micros=15)
    a[1, 1] = fetch_row(a[1, 0], 0, 1)
    c[0, 1] = fetch_seq(c[0, 0], 0, 1, 0)
    a[0, 2] = fetch_row(a[0, 3], 0, 3)
    c[2, 0] = fetch_seq(c[1, 0], 1, 0, 0)
    order = ((0, 0), (0, 1), (0, 3), (1, 0), (1, 1), (0, 2), (1, 3), (1, 2))
    early = row_values([a[o] for o in order[:4]], lookup)
    queries = row_queries(a[0, 0], wqk, horizontal_sigmoid_weights, limit)
    a, early, queries, c = hold(a, early, queries, c, micros=15)
    a[1, 2] = fetch_row(a[1, 1], 0, 1)
    a[1, 3] = fetch_row(a[1, 0], 0, 3)
    c[1, 1] = fetch_seq(c[0, 1], 1, 0, 0)
    c[3, 1] = fetch_seq(c[0, 1], 3, 0, 0)
    c[2, 1] = fetch_seq(c[2, 0], 0, 1, 0)
    middle = row_values([a[o] for o in order[4:6]], lookup)
    swap(*c)
    a, middle = hold(a, middle, micros=40)
    keys = {o: a[o] for o in order}
    rest = ([*early, *middle], bias, *queries, homolog_embedding, lookup)
    rest += (horizontal_merge_weights,)
    after_rows, send_0 = row_attention(keys, *rest, 0)
    after_rows, send_1 = row_attention(keys, *rest, 1, after_rows)
    column = (
        sequence_key_mask,
        cqk,
        vertical_lookup_weights,
        vertical_sigmoid_weights,
        vertical_merge_weights,
    )
    x_0, x_1 = (lax.all_to_all(x, "seq", 0, 0, tiled=True) for x in (send_0, send_1))
    done_0 = column_attention(x_0, *column, (after_rows,))
    x_1, done_0 = hold(x_1, done_0)
    done_1 = column_attention(x_1, *column)
    finals = [lax.all_to_all(x, "seq", 0, 0, tiled=True) for x in (done_0, done_1)]
    final = jnp.transpose(jnp.stack(finals), (2, 0, 1, 3, 4)).reshape(seqs, res, width)
    return after_rows, final


def solution(mesh):
    return jax.shard_map(
        per_device,
        mesh=mesh,
        in_specs=(P("seq", "res", None), P("res", "seq", None)) + (P(),) * 11,
        out_specs=(P("seq", "res", None), P("seq", "res", None)),
        check_vma=False,
    )
```

```python
import functools
import math

import jax
import jax.numpy as jnp
from jax import lax
from jax.experimental import pallas as pl
from jax.experimental.pallas import tpu as pltpu
from jax.sharding import PartitionSpec as P

HEADS = 8
GROUP = 4
LOG2E = math.log2(math.e)
MASKED = -1000000000.0
SAFE_SCORE = 100.0
BF16 = jnp.bfloat16
F32 = jnp.float32
NT = (((1,), (1,)), ((), ()))
VMEM_LIMIT = 60 * 2**20


def cost(micros):
    return pl.CostEstimate(flops=int(micros * 1e9), bytes_accessed=0, transcendentals=0)


def whole(*shape):
    return pl.BlockSpec(shape, lambda *_: (0,) * len(shape), pipeline_mode=pl.Buffered(1))


def right_half(w):
    rows, columns = w.shape
    return pl.BlockSpec((rows, columns // 2), lambda *_: (0, 1), pipeline_mode=pl.Buffered(1))


def layer_norm(x):
    center = x - jnp.mean(x, axis=-1, keepdims=True)
    spread = jnp.mean(center * center, axis=-1, keepdims=True)
    return center * lax.rsqrt(spread + 1e-05)


def after(*arrays):
    return list(arrays), [pl.BlockSpec(memory_space=pl.ANY)] * len(arrays)


def norm_kernel(x_ref, *refs):
    out_ref = refs[-1]
    for s in range(out_ref.shape[0]):
        out_ref[s] = layer_norm(x_ref[s].astype(F32)).astype(BF16)


def norm_rows(x, at, count, late=()):
    _, res, width = x.shape
    args, specs = after(*late)
    return pl.pallas_call(
        norm_kernel,
        grid=(1,),
        name="norm_rows",
        in_specs=[pl.BlockSpec((count, res, width), lambda i: (at // count, 0, 0))] + specs,
        out_specs=pl.BlockSpec((count, res, width), lambda i: (0, 0, 0)),
        out_shape=jax.ShapeDtypeStruct((count, res, width), BF16),
        cost_estimate=cost(2),
    )(x, *args)


def pair_kernel(x_ref, w_ref, mask_ref, *rest):
    out_ref, acc = rest[-2:]
    rows, keys, width = x_ref.shape
    half = rows // 2
    wide = 2 * width
    x = jnp.concatenate([x_ref[:half], x_ref[half:]], axis=-1).reshape(half * keys, wide)
    side = lax.broadcasted_iota(jnp.int32, (wide, wide), 0) // width
    same = side == lax.broadcasted_iota(jnp.int32, (wide, wide), 1) // width
    average = jnp.where(same, 1.0 / width, 0.0).astype(BF16)
    center = x.astype(F32) - jnp.dot(x, average, preferred_element_type=F32)
    square = (center * center).astype(BF16)
    center = center.astype(BF16)
    pick = jnp.where(
        lax.broadcasted_iota(jnp.int32, (2 * HEADS, wide), 0) // HEADS
        == lax.broadcasted_iota(jnp.int32, (2 * HEADS, wide), 1) // width,
        1.0 / width,
        0.0,
    ).astype(BF16)
    head_w = w_ref[...].astype(F32).T
    zero = jnp.zeros_like(head_w)
    head_w = jnp.concatenate(
        [
            jnp.concatenate([head_w, zero], axis=1),
            jnp.concatenate([zero, head_w], axis=1),
        ],
        axis=0,
    ).astype(BF16)
    for i in range(0, half, 2):
        here = slice(i * keys, (i + 2) * keys)
        both = lax.dot_general(head_w, center[here], NT, preferred_element_type=F32)
        spread = lax.dot_general(pick, square[here], NT, preferred_element_type=F32)
        both = both * lax.rsqrt(spread + 1e-05)
        for t in range(2):
            acc[i + t] = both[:HEADS, t * keys : (t + 1) * keys]
            acc[half + i + t] = both[HEADS:, t * keys : (t + 1) * keys]
    mask = mask_ref[...]
    here = mask_ref[pl.ds(lax.axis_index("seq"), 1), :]
    none = jnp.max(mask) <= 0
    keep = here > 0
    scale = jnp.where(none, 0.0, LOG2E)
    masked = jnp.where(none, 0.0, MASKED * LOG2E)
    for h in range(HEADS):
        b = jnp.where(keep, acc[:, h, :] * scale, masked)
        out_ref[h] = b.astype(BF16)


def pair_bias(pair, at, rows, head_w, mask, late=()):
    _, keys, width = pair.shape
    step = 64
    args, specs = after(*late)
    return pl.pallas_call(
        pair_kernel,
        grid=(rows // step,),
        name="pair_bias",
        in_specs=[
            pl.BlockSpec((step, keys, width), lambda i: (at // step + i, 0, 0)),
            whole(width, HEADS),
            whole(mask.shape[0] // keys, keys),
        ]
        + specs,
        out_specs=pl.BlockSpec((HEADS, step, keys), lambda i: (0, i, 0)),
        out_shape=jax.ShapeDtypeStruct((HEADS, rows, keys), BF16),
        scratch_shapes=[pltpu.VMEM((step, HEADS, keys), F32)],
        compiler_params=pltpu.CompilerParams(vmem_limit_bytes=VMEM_LIMIT),
        cost_estimate=cost(6),
    )(pair, head_w, mask.reshape(-1, keys), *args)


def head_lanes(rows, h, o):
    lane = lax.broadcasted_iota(jnp.int32, (rows, 128), 1) // 32
    return jnp.where(lane == h % 4, o, 0.0)


def query_kernel(own_ref, wqk_ref, wg_ref, limit_ref, q_ref, gate_ref, fast_ref):
    _, rows, width = own_ref.shape
    own = own_ref[0]
    largest = jnp.zeros((rows, 1), F32)
    for h in range(HEADS):
        q = jnp.dot(own, wqk_ref[:, h * width : (h + 1) * width], preferred_element_type=F32)
        largest = jnp.maximum(largest, jnp.sum(q * q, axis=-1, keepdims=True))
        q_ref[0, h] = q.astype(BF16)
    gate_ref[0] = jax.nn.sigmoid(jnp.dot(own, wg_ref[...], preferred_element_type=F32))
    fast = (jnp.max(largest) < limit_ref[0]).astype(jnp.int32)

    @pl.when(pl.program_id(0) == 0)
    def _():
        fast_ref[0] = 1

    fast_ref[0] = fast_ref[0] * fast


def row_queries(own, wqk, wg, limit):
    seqs, rows, width = own.shape
    smem = pl.BlockSpec(memory_space=pltpu.SMEM)
    return pl.pallas_call(
        query_kernel,
        grid=(seqs,),
        name="row_queries",
        in_specs=[
            pl.BlockSpec((1, rows, width), lambda s: (s, 0, 0)),
            whole(*wqk.shape),
            whole(*wg.shape),
            smem,
        ],
        out_specs=[
            pl.BlockSpec((1, HEADS, rows, width), lambda s: (s, 0, 0, 0)),
            pl.BlockSpec((1, rows, width), lambda s: (s, 0, 0)),
            smem,
        ],
        out_shape=[
            jax.ShapeDtypeStruct((seqs, HEADS, rows, width), BF16),
            jax.ShapeDtypeStruct((seqs, rows, width), F32),
            jax.ShapeDtypeStruct((1,), jnp.int32),
        ],
        cost_estimate=cost(6),
    )(own, wqk, wg, limit)


def value_kernel(*refs):
    n = len(refs) // 2
    for x, out in zip(refs[:n], refs[n + 1 :]):
        out[0] = jnp.dot(x[0], refs[n][...], preferred_element_type=F32).astype(BF16)


def row_values(blocks, wv):
    seqs, rows, width = blocks[0].shape
    one = pl.BlockSpec((1, rows, width), lambda s: (s, 0, 0))
    return pl.pallas_call(
        value_kernel,
        grid=(seqs,),
        name="row_values",
        in_specs=[one] * len(blocks) + [right_half(wv)],
        out_specs=[one] * len(blocks),
        out_shape=[jax.ShapeDtypeStruct(x.shape, BF16) for x in blocks],
        cost_estimate=cost(1.5 * len(blocks)),
    )(*blocks, wv)


def row_kernel(spec, *refs):
    offsets, n_values, places = spec
    n_keys = len(offsets)
    refs = list(refs)
    take = lambda n: [refs.pop(0) for _ in range(n)]
    keys, values = take(n_keys), take(n_values)
    bias_in = take(len(places))
    q_ref, gate_ref, emb_ref, fast_ref, wv_ref, wm_ref = take(6)
    out_ref, send_ref, bias, late, sems = refs
    each, block, width = keys[0].shape
    _, heads, rows, tile = bias.shape
    per = block // tile
    pack = max(1, block // rows)
    first = pl.program_id(0) == 0
    seq = lax.axis_index("seq")
    res = lax.axis_index("res")

    def copies():
        n = 0
        for ref, group in zip(bias_in, places):
            for i, (dy, dz, dc) in enumerate(group):
                place = (
                    lax.rem(seq // 4 + dy, 4) * 4
                    + lax.rem(seq // 2 + dz, 2) * 2
                    + lax.rem(seq + dc, 2)
                )
                yield pltpu.make_async_copy(ref.at[i], bias.at[place], sems.at[n])
                n += 1

    @pl.when(first)
    def _():
        for c in copies():
            c.start()

    for i in range(each):
        for k in range(n_values, n_keys):
            v = jnp.dot(keys[k][i], wv_ref[...], preferred_element_type=F32)
            late[i, k - n_values] = v.astype(BF16)

    @pl.when(first)
    def _():
        for c in copies():
            c.wait()

    ones = jnp.ones((block, 128), BF16)

    def value(i, g, k):
        lanes = slice(g * 128, (g + 1) * 128)
        v = values[k][i, :, lanes] if k < n_values else late[i, k - n_values, :, lanes]
        return jnp.concatenate([v, ones], axis=1)

    at = [
        (lax.rem(res // 4 + dz, 2) * 4 + lax.rem(res + dx, 4)) * per for dz, dx in offsets
    ]

    def scores(i, h, k):
        q = q_ref[i, h : h + pack].reshape(pack * rows, width)
        s = lax.dot_general(q, keys[k][i], NT, preferred_element_type=F32)
        b = [bias[at[k] + t, h : h + pack].reshape(pack * rows, tile) for t in range(per)]
        return s + jnp.concatenate(b, axis=1).astype(F32)

    def mix(i, with_top):
        halves = []
        for g in range(2):
            total = None
            for h in range(g * GROUP, (g + 1) * GROUP, pack):
                top = None
                if with_top:
                    tops = [
                        jnp.max(scores(i, h, k), axis=-1, keepdims=True) for k in range(n_keys)
                    ]
                    top = functools.reduce(jnp.maximum, tops)
                u = None
                for k in range(n_keys):
                    s = scores(i, h, k)
                    e = jnp.exp2(s - top if with_top else s).astype(BF16)
                    d = jnp.dot(e, value(i, g, k), preferred_element_type=F32)
                    u = d if u is None else u + d
                o = u[:, :128] / u[:, 128:]
                for j in range(pack):
                    part = head_lanes(rows, h + j, o[j * rows : (j + 1) * rows])
                    total = part if total is None else total + part
            halves.append(total)
        gated = (jnp.concatenate(halves, axis=1) * gate_ref[i]).astype(BF16)
        update = jnp.dot(gated, wm_ref[...], preferred_element_type=F32)
        result = (emb_ref[i].astype(F32) + update).astype(BF16)
        out_ref[i] = result
        send_ref[:, i] = result.reshape(send_ref.shape[0], send_ref.shape[2], width)

    fast = fast_ref[0] > 0

    @pl.when(fast)
    def _():
        for i in range(each):
            mix(i, False)

    @pl.when(jnp.logical_not(fast))
    def _():
        lax.fori_loop(0, each, lambda i, carry: (mix(i, True), carry)[1], 0)


def row_attention(keys, values, bias, queries, gate, fast, emb, wv, wm):
    offsets, places = tuple(keys), tuple(bias)
    seqs, block, width = emb.shape
    _, heads, rows, tile = bias[places[0]].shape
    tiles = sum(len(group) for group in places)
    parts = lax.axis_size("seq")
    part = rows // parts
    each = 1
    mine = pl.BlockSpec((each, rows, width), lambda s: (s, 0, 0))
    args = [*keys.values(), *values, *bias.values(), queries, gate, emb, fast, wv, wm]
    specs = [pl.BlockSpec((each, block, width), lambda s: (s, 0, 0))] * (len(keys) + len(values))
    specs += [pl.BlockSpec(memory_space=pl.ANY)] * len(bias)
    specs += [pl.BlockSpec((each, heads, rows, width), lambda s: (s, 0, 0, 0)), mine, mine]
    specs += [pl.BlockSpec(memory_space=pltpu.SMEM), right_half(wv), whole(*wm.shape)]
    spec = (offsets, len(values), places)
    return pl.pallas_call(
        functools.partial(row_kernel, spec),
        grid=(seqs // each,),
        name="row_attention",
        in_specs=specs,
        out_specs=[mine, pl.BlockSpec((parts, each, part, width), lambda s: (0, s, 0, 0))],
        out_shape=[
            jax.ShapeDtypeStruct(emb.shape, BF16),
            jax.ShapeDtypeStruct((parts, seqs, part, width), BF16),
        ],
        scratch_shapes=[
            pltpu.VMEM((tiles, heads, rows, tile), BF16),
            pltpu.VMEM((each, len(keys) - len(values), block, width), BF16),
            pltpu.SemaphoreType.DMA((tiles,)),
        ],
        compiler_params=pltpu.CompilerParams(vmem_limit_bytes=VMEM_LIMIT),
        cost_estimate=cost(45),
    )(*args)


def column_kernel(
    x_ref, mask_ref, wqk_ref, wv_ref, wg_ref, wm_ref, *rest
):
    out_ref, raw, normed, done, qs = rest[-5:]
    groups, each, res, width = x_ref.shape
    seqs = groups * each
    x = x_ref[...].astype(F32)
    raw[...] = x
    normed[...] = layer_norm(x)
    ones = jnp.ones((seqs, 128), BF16)
    mask = mask_ref[...] > 0
    span = range(res)
    n = [normed[:, :, r, :].reshape(seqs, width).astype(BF16) for r in span]
    flat = jnp.concatenate(n, axis=0)
    v = jnp.dot(flat, wv_ref[...], preferred_element_type=F32).astype(BF16)
    gate = jax.nn.sigmoid(jnp.dot(flat, wg_ref[...], preferred_element_type=F32))
    for h in range(HEADS):
        q = jnp.dot(flat, wqk_ref[:, h * width : (h + 1) * width], preferred_element_type=F32)
        q = q.astype(BF16)
        for r in span:
            qs[r, h // 4, (h % 4) * seqs : (h % 4 + 1) * seqs] = q[r * seqs : (r + 1) * seqs]
    mixed = []
    for r in span:
        halves = []
        for g in range(2):
            s = lax.dot_general(qs[r, g], n[r], NT, preferred_element_type=F32)
            s = jnp.where(mask, s, MASKED)
            e = jnp.exp2(s - jnp.max(s, axis=-1, keepdims=True)).astype(BF16)
            va = jnp.concatenate(
                [v[r * seqs : (r + 1) * seqs, g * 128 : (g + 1) * 128], ones], axis=1
            )
            u = jnp.dot(e, va, preferred_element_type=F32)
            o = u[:, :128] / u[:, 128:]
            halves.append(
                sum(head_lanes(seqs, h, o[h * seqs : (h + 1) * seqs]) for h in range(4))
            )
        mixed.append(jnp.concatenate(halves, axis=1))
    gated = (jnp.concatenate(mixed, axis=0) * gate).astype(BF16)
    update = jnp.dot(gated, wm_ref[...], preferred_element_type=F32)
    for r in span:
        before = raw[:, :, r, :]
        done[:, :, r, :] = before + update[r * seqs : (r + 1) * seqs].reshape(before.shape)
    out_ref[...] = done[...].astype(BF16)


def column_attention(x, mask, wqk, wv, wg, wm, late=()):
    args, specs = after(*late)
    return pl.pallas_call(
        column_kernel,
        grid=(1,),
        name="column_attention",
        in_specs=[whole(*x.shape), whole(1, mask.shape[0]), whole(*wqk.shape), right_half(wv)]
        + [whole(*wg.shape), whole(*wm.shape)]
        + specs,
        out_specs=whole(*x.shape),
        out_shape=jax.ShapeDtypeStruct(x.shape, BF16),
        scratch_shapes=[pltpu.VMEM(x.shape, F32)] * 3
        + [pltpu.VMEM((x.shape[2], 2, 4 * x.shape[0] * x.shape[1], x.shape[3]), BF16)],
        compiler_params=pltpu.CompilerParams(vmem_limit_bytes=VMEM_LIMIT),
        cost_estimate=cost(8),
    )(x, mask.reshape(1, -1), wqk, wv, wg, wm, *args)


def fold_kernel(
    mask_ref, head_ref, rq_ref, rkv_ref, cq_ref, ckv_ref, wqk_ref, cqk_ref, limit_ref
):
    width = rq_ref.shape[0]
    size = width // HEADS
    factor = LOG2E / math.sqrt(size)
    some = jnp.max(mask_ref[...]) > 0
    lane = lax.broadcasted_iota(jnp.int32, (width, width), 1) // size
    for q_ref, k_ref, out_ref, scale in (
        (rq_ref, rkv_ref, wqk_ref, jnp.where(some, factor, 0.0)),
        (cq_ref, ckv_ref, cqk_ref, factor),
    ):
        q, k = q_ref[...], k_ref[:, :width]
        for h in range(HEADS):
            one = jnp.where(lane == h, q, jnp.zeros_like(q))
            both = lax.dot_general(one, k, NT, preferred_element_type=F32)
            out_ref[:, h * width : (h + 1) * width] = (both * scale).astype(BF16)
    head = head_ref[...].astype(F32)
    norm = jnp.max(jnp.sqrt(jnp.sum(head * head, axis=0, keepdims=True)))
    room = SAFE_SCORE - 1.02 * LOG2E * math.sqrt(head.shape[0]) * norm
    room = jnp.maximum(room, 0.0) / (1.02 * math.sqrt(width))
    limit_ref[0] = room * room


def fold_weights(mask, head_w, rq, rkv, cq, ckv):
    width = rq.shape[0]
    vmem = pl.BlockSpec(memory_space=pltpu.VMEM)
    return pl.pallas_call(
        fold_kernel,
        name="fold_weights",
        out_specs=[vmem, vmem, pl.BlockSpec(memory_space=pltpu.SMEM)],
        out_shape=[jax.ShapeDtypeStruct((width, HEADS * width), BF16)] * 2
        + [jax.ShapeDtypeStruct((1,), F32)],
        cost_estimate=cost(3),
    )(mask, head_w, rq, rkv, cq, ckv)


def fetch_seq(x, dy, dz, dc):
    pairs = [
        (((y + dy) % 4) * 4 + ((z + dz) % 2) * 2 + (c + dc) % 2, y * 4 + z * 2 + c)
        for y in range(4)
        for z in range(2)
        for c in range(2)
    ]
    return lax.ppermute(x, "seq", pairs)


def fetch_row(x, dz, dx):
    pairs = [
        (((z + dz) % 2) * 4 + (i + dx) % 4, z * 4 + i) for z in range(2) for i in range(4)
    ]
    return lax.ppermute(x, "res", pairs)


def pack_kernel(*refs):
    for i, ref in enumerate(refs[:-1]):
        refs[-1][i] = ref[...]


def pack_blocks(blocks):
    first, *others = blocks[0].shape
    step = first // 4
    return pl.pallas_call(
        pack_kernel,
        grid=(4,),
        name="pack_blocks",
        in_specs=[pl.BlockSpec((step, *others), lambda i: (i, 0, 0))] * len(blocks),
        out_specs=pl.BlockSpec((len(blocks), step, *others), lambda i: (0, i, 0, 0)),
        out_shape=jax.ShapeDtypeStruct((len(blocks), first, *others), blocks[0].dtype),
        cost_estimate=cost(2),
    )(*blocks)


def hold_kernel(*refs):
    pass


def hold(*trees, micros=1):
    boxes = [dict(zip(range(len(t)), t.values())) if isinstance(t, dict) else t for t in trees]
    flat, tree = jax.tree.flatten(boxes)
    any_ = pl.BlockSpec(memory_space=pl.ANY)
    out = pl.pallas_call(
        hold_kernel,
        name="step_done",
        in_specs=[any_] * len(flat),
        out_specs=[any_] * len(flat),
        out_shape=[jax.ShapeDtypeStruct(x.shape, x.dtype) for x in flat],
        input_output_aliases={i: i for i in range(len(flat))},
        cost_estimate=cost(micros),
    )(*flat)
    out = jax.tree.unflatten(tree, out)
    return [dict(zip(t, o.values())) if isinstance(t, dict) else o for t, o in zip(trees, out)]


def per_device(
    homolog_embedding,
    pair_features,
    sequence_key_mask,
    residue_key_mask,
    pair_head_bias_matrix,
    horizontal_probe_weights,
    horizontal_lookup_weights,
    horizontal_sigmoid_weights,
    horizontal_merge_weights,
    column_query_matrix,
    vertical_lookup_weights,
    vertical_sigmoid_weights,
    vertical_merge_weights,
):
    seqs, res, width = homolog_embedding.shape
    groups = lax.axis_size("seq")
    wqk, cqk, limit = fold_weights(
        residue_key_mask.reshape(16, -1),
        pair_head_bias_matrix,
        horizontal_probe_weights,
        horizontal_lookup_weights,
        column_query_matrix,
        vertical_lookup_weights,
    )
    lookup = horizontal_lookup_weights
    a, c = {}, {}
    a[0, 0] = norm_rows(homolog_embedding, 0, seqs)
    a[0, 1] = fetch_row(a[0, 0], 0, 1)
    a[0, 3] = fetch_row(a[0, 0], 0, 3)
    a[1, 0] = fetch_row(a[0, 0], 1, 0)
    c[0, 0] = pair_bias(
        pair_features, 0, res, pair_head_bias_matrix, residue_key_mask, (a[0, 0],)
    )
    c[1, 0] = fetch_seq(c[0, 0], 1, 0, 0)
    c[3, 0] = fetch_seq(c[0, 0], 3, 0, 0)
    bias = {}

    def swap(*offsets):
        both = c[offsets[0]][None] if len(offsets) == 1 else pack_blocks([c[o] for o in offsets])
        bias[tuple((*o, 0) for o in offsets)] = both
        bias[tuple((*o, 1) for o in offsets)] = fetch_seq(both, 0, 0, 1)

    (a,) = hold(a, micros=15)
    a[1, 1] = fetch_row(a[1, 0], 0, 1)
    c[0, 1] = fetch_seq(c[0, 0], 0, 1, 0)
    a[0, 2] = fetch_row(a[0, 3], 0, 3)
    c[2, 0] = fetch_seq(c[1, 0], 1, 0, 0)
    order = ((0, 0), (0, 1), (0, 3), (1, 0), (1, 1), (0, 2), (1, 3), (1, 2))
    early = row_values([a[o] for o in order[:4]], lookup)
    queries = row_queries(a[0, 0], wqk, horizontal_sigmoid_weights, limit)
    a, early, queries, c = hold(a, early, queries, c, micros=15)
    a[1, 2] = fetch_row(a[1, 1], 0, 1)
    a[1, 3] = fetch_row(a[1, 0], 0, 3)
    c[1, 1] = fetch_seq(c[0, 1], 1, 0, 0)
    c[3, 1] = fetch_seq(c[0, 1], 3, 0, 0)
    c[2, 1] = fetch_seq(c[2, 0], 0, 1, 0)
    middle = row_values([a[o] for o in order[4:6]], lookup)
    swap(*c)
    a, middle = hold(a, middle, micros=40)
    keys = {o: a[o] for o in order}
    rest = ([*early, *middle], bias, *queries, homolog_embedding, lookup)
    rest += (horizontal_merge_weights,)
    after_rows, send = row_attention(keys, *rest)
    result = column_attention(
        lax.all_to_all(send, "seq", 0, 0, tiled=True),
        sequence_key_mask,
        cqk,
        vertical_lookup_weights,
        vertical_sigmoid_weights,
        vertical_merge_weights,
    )
    back = lax.all_to_all(result, "seq", 0, 0, tiled=True)
    return after_rows, jnp.transpose(back, (1, 0, 2, 3)).reshape(seqs, res, width)


def solution(mesh):
    return jax.shard_map(
        per_device,
        mesh=mesh,
        in_specs=(P("seq", "res", None), P("res", "seq", None)) + (P(),) * 11,
        out_specs=(P("seq", "res", None), P("seq", "res", None)),
        check_vma=False,
    )
```

```python
import functools
import math

import jax
import jax.numpy as jnp
from jax import lax
from jax.experimental import pallas as pl
from jax.experimental.pallas import tpu as pltpu
from jax.sharding import PartitionSpec as P

HEADS = 8
GROUP = 4
LOG2E = math.log2(math.e)
MASKED = -1000000000.0
SAFE_SCORE = 100.0
BF16 = jnp.bfloat16
F32 = jnp.float32
NT = (((1,), (1,)), ((), ()))
VMEM_LIMIT = 60 * 2**20


def cost(micros):
    return pl.CostEstimate(flops=int(micros * 1e9), bytes_accessed=0, transcendentals=0)


def whole(*shape):
    return pl.BlockSpec(shape, lambda *_: (0,) * len(shape), pipeline_mode=pl.Buffered(1))


def right_half(w):
    rows, columns = w.shape
    return pl.BlockSpec((rows, columns // 2), lambda *_: (0, 1), pipeline_mode=pl.Buffered(1))


def layer_norm(x):
    center = x - jnp.mean(x, axis=-1, keepdims=True)
    spread = jnp.mean(center * center, axis=-1, keepdims=True)
    return center * lax.rsqrt(spread + 1e-05)


def after(*arrays):
    return list(arrays), [pl.BlockSpec(memory_space=pl.ANY)] * len(arrays)


def norm_kernel(x_ref, *refs):
    out_ref = refs[-1]
    for s in range(out_ref.shape[0]):
        out_ref[s] = layer_norm(x_ref[s].astype(F32)).astype(BF16)


def norm_rows(x, at, count, late=()):
    _, res, width = x.shape
    args, specs = after(*late)
    return pl.pallas_call(
        norm_kernel,
        grid=(1,),
        name="norm_rows",
        in_specs=[pl.BlockSpec((count, res, width), lambda i: (at // count, 0, 0))] + specs,
        out_specs=pl.BlockSpec((count, res, width), lambda i: (0, 0, 0)),
        out_shape=jax.ShapeDtypeStruct((count, res, width), BF16),
        cost_estimate=cost(2),
    )(x, *args)


def pair_kernel(x_ref, w_ref, mask_ref, *rest):
    out_ref, acc = rest[-2:]
    rows, keys, width = x_ref.shape
    half = rows // 2
    wide = 2 * width
    x = jnp.concatenate([x_ref[:half], x_ref[half:]], axis=-1).reshape(half * keys, wide)
    side = lax.broadcasted_iota(jnp.int32, (wide, wide), 0) // width
    same = side == lax.broadcasted_iota(jnp.int32, (wide, wide), 1) // width
    average = jnp.where(same, 1.0 / width, 0.0).astype(BF16)
    center = x.astype(F32) - jnp.dot(x, average, preferred_element_type=F32)
    square = (center * center).astype(BF16)
    center = center.astype(BF16)
    pick = jnp.where(
        lax.broadcasted_iota(jnp.int32, (2 * HEADS, wide), 0) // HEADS
        == lax.broadcasted_iota(jnp.int32, (2 * HEADS, wide), 1) // width,
        1.0 / width,
        0.0,
    ).astype(BF16)
    head_w = w_ref[...].astype(F32).T
    zero = jnp.zeros_like(head_w)
    head_w = jnp.concatenate(
        [
            jnp.concatenate([head_w, zero], axis=1),
            jnp.concatenate([zero, head_w], axis=1),
        ],
        axis=0,
    ).astype(BF16)
    for i in range(0, half, 2):
        here = slice(i * keys, (i + 2) * keys)
        both = lax.dot_general(head_w, center[here], NT, preferred_element_type=F32)
        spread = lax.dot_general(pick, square[here], NT, preferred_element_type=F32)
        both = both * lax.rsqrt(spread + 1e-05)
        for t in range(2):
            acc[i + t] = both[:HEADS, t * keys : (t + 1) * keys]
            acc[half + i + t] = both[HEADS:, t * keys : (t + 1) * keys]
    mask = mask_ref[...]
    here = mask_ref[pl.ds(lax.axis_index("seq"), 1), :]
    none = jnp.max(mask) <= 0
    keep = here > 0
    scale = jnp.where(none, 0.0, LOG2E)
    masked = jnp.where(none, 0.0, MASKED * LOG2E)
    for h in range(HEADS):
        b = jnp.where(keep, acc[:, h, :] * scale, masked)
        out_ref[h] = b.astype(BF16)


def pair_bias(pair, at, rows, head_w, mask, late=()):
    _, keys, width = pair.shape
    step = 64
    args, specs = after(*late)
    return pl.pallas_call(
        pair_kernel,
        grid=(rows // step,),
        name="pair_bias",
        in_specs=[
            pl.BlockSpec((step, keys, width), lambda i: (at // step + i, 0, 0)),
            whole(width, HEADS),
            whole(mask.shape[0] // keys, keys),
        ]
        + specs,
        out_specs=pl.BlockSpec((HEADS, step, keys), lambda i: (0, i, 0)),
        out_shape=jax.ShapeDtypeStruct((HEADS, rows, keys), BF16),
        scratch_shapes=[pltpu.VMEM((step, HEADS, keys), F32)],
        compiler_params=pltpu.CompilerParams(vmem_limit_bytes=VMEM_LIMIT),
        cost_estimate=cost(6),
    )(pair, head_w, mask.reshape(-1, keys), *args)


def head_lanes(rows, h, o):
    lane = lax.broadcasted_iota(jnp.int32, (rows, 128), 1) // 32
    return jnp.where(lane == h % 4, o, 0.0)


def query_kernel(own_ref, wqk_ref, wg_ref, limit_ref, q_ref, gate_ref, fast_ref):
    _, rows, width = own_ref.shape
    own = own_ref[0]
    largest = jnp.zeros((rows, 1), F32)
    for h in range(HEADS):
        q = jnp.dot(own, wqk_ref[:, h * width : (h + 1) * width], preferred_element_type=F32)
        largest = jnp.maximum(largest, jnp.sum(q * q, axis=-1, keepdims=True))
        q_ref[0, h] = q.astype(BF16)
    gate_ref[0] = jax.nn.sigmoid(jnp.dot(own, wg_ref[...], preferred_element_type=F32))
    fast = (jnp.max(largest) < limit_ref[0]).astype(jnp.int32)

    @pl.when(pl.program_id(0) == 0)
    def _():
        fast_ref[0] = 1

    fast_ref[0] = fast_ref[0] * fast


def row_queries(own, wqk, wg, limit):
    seqs, rows, width = own.shape
    smem = pl.BlockSpec(memory_space=pltpu.SMEM)
    return pl.pallas_call(
        query_kernel,
        grid=(seqs,),
        name="row_queries",
        in_specs=[
            pl.BlockSpec((1, rows, width), lambda s: (s, 0, 0)),
            whole(*wqk.shape),
            whole(*wg.shape),
            smem,
        ],
        out_specs=[
            pl.BlockSpec((1, HEADS, rows, width), lambda s: (s, 0, 0, 0)),
            pl.BlockSpec((1, rows, width), lambda s: (s, 0, 0)),
            smem,
        ],
        out_shape=[
            jax.ShapeDtypeStruct((seqs, HEADS, rows, width), BF16),
            jax.ShapeDtypeStruct((seqs, rows, width), F32),
            jax.ShapeDtypeStruct((1,), jnp.int32),
        ],
        cost_estimate=cost(6),
    )(own, wqk, wg, limit)


def value_kernel(*refs):
    n = len(refs) // 2
    for x, out in zip(refs[:n], refs[n + 1 :]):
        out[0] = jnp.dot(x[0], refs[n][...], preferred_element_type=F32).astype(BF16)


def row_values(blocks, wv):
    seqs, rows, width = blocks[0].shape
    one = pl.BlockSpec((1, rows, width), lambda s: (s, 0, 0))
    return pl.pallas_call(
        value_kernel,
        grid=(seqs,),
        name="row_values",
        in_specs=[one] * len(blocks) + [right_half(wv)],
        out_specs=[one] * len(blocks),
        out_shape=[jax.ShapeDtypeStruct(x.shape, BF16) for x in blocks],
        cost_estimate=cost(1.5 * len(blocks)),
    )(*blocks, wv)


def row_kernel(spec, *refs):
    offsets, n_values, places = spec
    n_keys = len(offsets)
    refs = list(refs)
    take = lambda n: [refs.pop(0) for _ in range(n)]
    keys, values = take(n_keys), take(n_values)
    bias_in = take(len(places))
    q_ref, gate_ref, emb_ref, fast_ref, wv_ref, wm_ref = take(6)
    out_ref, send_ref, bias, late, sems = refs
    each, block, width = keys[0].shape
    _, heads, rows, tile = bias.shape
    per = block // tile
    pack = max(1, block // rows)
    first = pl.program_id(0) == 0
    seq = lax.axis_index("seq")
    res = lax.axis_index("res")

    def copies():
        n = 0
        for ref, group in zip(bias_in, places):
            for i, (dy, dz, dc) in enumerate(group):
                place = (
                    lax.rem(seq // 4 + dy, 4) * 4
                    + lax.rem(seq // 2 + dz, 2) * 2
                    + lax.rem(seq + dc, 2)
                )
                yield pltpu.make_async_copy(ref.at[i], bias.at[place], sems.at[n])
                n += 1

    @pl.when(first)
    def _():
        for c in copies():
            c.start()

    for i in range(each):
        for k in range(n_values, n_keys):
            v = jnp.dot(keys[k][i], wv_ref[...], preferred_element_type=F32)
            late[i, k - n_values] = v.astype(BF16)

    @pl.when(first)
    def _():
        for c in copies():
            c.wait()

    ones = jnp.ones((block, 128), BF16)

    def value(i, g, k):
        lanes = slice(g * 128, (g + 1) * 128)
        v = values[k][i, :, lanes] if k < n_values else late[i, k - n_values, :, lanes]
        return jnp.concatenate([v, ones], axis=1)

    at = [
        (lax.rem(res // 4 + dz, 2) * 4 + lax.rem(res + dx, 4)) * per for dz, dx in offsets
    ]

    def scores(i, h, k):
        q = q_ref[i, h : h + pack].reshape(pack * rows, width)
        s = lax.dot_general(q, keys[k][i], NT, preferred_element_type=F32)
        b = [bias[at[k] + t, h : h + pack].reshape(pack * rows, tile) for t in range(per)]
        return s + jnp.concatenate(b, axis=1).astype(F32)

    def pair_of_heads(i, h, with_top):
        g = h // GROUP
        top = None
        if with_top:
            tops = [jnp.max(scores(i, h, k), axis=-1, keepdims=True) for k in range(n_keys)]
            top = functools.reduce(jnp.maximum, tops)
        u = None
        for k in range(n_keys):
            s = scores(i, h, k)
            e = jnp.exp2(s - top if with_top else s).astype(BF16)
            d = jnp.dot(e, value(i, g, k), preferred_element_type=F32)
            u = d if u is None else u + d
        o = u[:, :128] / u[:, 128:]
        return sum(head_lanes(rows, h + j, o[j * rows : (j + 1) * rows]) for j in range(pack))

    def merge(i, parts):
        n = len(parts) // 2
        mixed = jnp.concatenate([sum(parts[:n]), sum(parts[n:])], axis=1)
        gated = (mixed * gate_ref[i]).astype(BF16)
        update = jnp.dot(gated, wm_ref[...], preferred_element_type=F32)
        result = (emb_ref[i].astype(F32) + update).astype(BF16)
        out_ref[i] = result
        send_ref[:, i] = result.reshape(send_ref.shape[0], send_ref.shape[2], width)

    fast = fast_ref[0] > 0

    @pl.when(fast)
    def _():
        before = None
        for i in range(each):
            parts = []
            for h in range(0, heads, pack):
                parts.append(pair_of_heads(i, h, False))
                if before is not None:
                    merge(*before)
                    before = None
            before = i, parts
        merge(*before)

    @pl.when(jnp.logical_not(fast))
    def _():
        def one(i, carry):
            merge(i, [pair_of_heads(i, h, True) for h in range(0, heads, pack)])
            return carry

        lax.fori_loop(0, each, one, 0)


def row_attention(keys, values, bias, queries, gate, fast, emb, wv, wm):
    offsets, places = tuple(keys), tuple(bias)
    seqs, block, width = emb.shape
    _, heads, rows, tile = bias[places[0]].shape
    tiles = sum(len(group) for group in places)
    parts = lax.axis_size("seq")
    part = rows // parts
    each = 2
    mine = pl.BlockSpec((each, rows, width), lambda s: (s, 0, 0))
    args = [*keys.values(), *values, *bias.values(), queries, gate, emb, fast, wv, wm]
    specs = [pl.BlockSpec((each, block, width), lambda s: (s, 0, 0))] * (len(keys) + len(values))
    specs += [pl.BlockSpec(memory_space=pl.ANY)] * len(bias)
    specs += [pl.BlockSpec((each, heads, rows, width), lambda s: (s, 0, 0, 0)), mine, mine]
    specs += [pl.BlockSpec(memory_space=pltpu.SMEM), right_half(wv), whole(*wm.shape)]
    spec = (offsets, len(values), places)
    return pl.pallas_call(
        functools.partial(row_kernel, spec),
        grid=(seqs // each,),
        name="row_attention",
        in_specs=specs,
        out_specs=[mine, pl.BlockSpec((parts, each, part, width), lambda s: (0, s, 0, 0))],
        out_shape=[
            jax.ShapeDtypeStruct(emb.shape, BF16),
            jax.ShapeDtypeStruct((parts, seqs, part, width), BF16),
        ],
        scratch_shapes=[
            pltpu.VMEM((tiles, heads, rows, tile), BF16),
            pltpu.VMEM((each, len(keys) - len(values), block, width), BF16),
            pltpu.SemaphoreType.DMA((tiles,)),
        ],
        compiler_params=pltpu.CompilerParams(vmem_limit_bytes=VMEM_LIMIT),
        cost_estimate=cost(45),
    )(*args)


def column_kernel(
    x_ref, mask_ref, wqk_ref, wv_ref, wg_ref, wm_ref, *rest
):
    out_ref, raw, normed, done, qs = rest[-5:]
    groups, each, res, width = x_ref.shape
    seqs = groups * each
    x = x_ref[...].astype(F32)
    raw[...] = x
    normed[...] = layer_norm(x)
    ones = jnp.ones((seqs, 128), BF16)
    mask = mask_ref[...] > 0
    span = range(res)
    n = [normed[:, :, r, :].reshape(seqs, width).astype(BF16) for r in span]
    flat = jnp.concatenate(n, axis=0)
    v = jnp.dot(flat, wv_ref[...], preferred_element_type=F32).astype(BF16)
    gate = jax.nn.sigmoid(jnp.dot(flat, wg_ref[...], preferred_element_type=F32))
    for h in range(HEADS):
        q = jnp.dot(flat, wqk_ref[:, h * width : (h + 1) * width], preferred_element_type=F32)
        q = q.astype(BF16)
        for r in span:
            qs[r, h // 4, (h % 4) * seqs : (h % 4 + 1) * seqs] = q[r * seqs : (r + 1) * seqs]
    mixed = []
    for r in span:
        halves = []
        for g in range(2):
            s = lax.dot_general(qs[r, g], n[r], NT, preferred_element_type=F32)
            s = jnp.where(mask, s, MASKED)
            e = jnp.exp2(s - jnp.max(s, axis=-1, keepdims=True)).astype(BF16)
            va = jnp.concatenate(
                [v[r * seqs : (r + 1) * seqs, g * 128 : (g + 1) * 128], ones], axis=1
            )
            u = jnp.dot(e, va, preferred_element_type=F32)
            o = u[:, :128] / u[:, 128:]
            halves.append(
                sum(head_lanes(seqs, h, o[h * seqs : (h + 1) * seqs]) for h in range(4))
            )
        mixed.append(jnp.concatenate(halves, axis=1))
    gated = (jnp.concatenate(mixed, axis=0) * gate).astype(BF16)
    update = jnp.dot(gated, wm_ref[...], preferred_element_type=F32)
    for r in span:
        before = raw[:, :, r, :]
        done[:, :, r, :] = before + update[r * seqs : (r + 1) * seqs].reshape(before.shape)
    out_ref[...] = done[...].astype(BF16)


def column_attention(x, mask, wqk, wv, wg, wm, late=()):
    args, specs = after(*late)
    return pl.pallas_call(
        column_kernel,
        grid=(1,),
        name="column_attention",
        in_specs=[whole(*x.shape), whole(1, mask.shape[0]), whole(*wqk.shape), right_half(wv)]
        + [whole(*wg.shape), whole(*wm.shape)]
        + specs,
        out_specs=whole(*x.shape),
        out_shape=jax.ShapeDtypeStruct(x.shape, BF16),
        scratch_shapes=[pltpu.VMEM(x.shape, F32)] * 3
        + [pltpu.VMEM((x.shape[2], 2, 4 * x.shape[0] * x.shape[1], x.shape[3]), BF16)],
        compiler_params=pltpu.CompilerParams(vmem_limit_bytes=VMEM_LIMIT),
        cost_estimate=cost(8),
    )(x, mask.reshape(1, -1), wqk, wv, wg, wm, *args)


def fold_kernel(
    mask_ref, head_ref, rq_ref, rkv_ref, cq_ref, ckv_ref, wqk_ref, cqk_ref, limit_ref
):
    width = rq_ref.shape[0]
    size = width // HEADS
    factor = LOG2E / math.sqrt(size)
    some = jnp.max(mask_ref[...]) > 0
    lane = lax.broadcasted_iota(jnp.int32, (width, width), 1) // size
    for q_ref, k_ref, out_ref, scale in (
        (rq_ref, rkv_ref, wqk_ref, jnp.where(some, factor, 0.0)),
        (cq_ref, ckv_ref, cqk_ref, factor),
    ):
        q, k = q_ref[...], k_ref[:, :width]
        for h in range(HEADS):
            one = jnp.where(lane == h, q, jnp.zeros_like(q))
            both = lax.dot_general(one, k, NT, preferred_element_type=F32)
            out_ref[:, h * width : (h + 1) * width] = (both * scale).astype(BF16)
    head = head_ref[...].astype(F32)
    norm = jnp.max(jnp.sqrt(jnp.sum(head * head, axis=0, keepdims=True)))
    room = SAFE_SCORE - 1.02 * LOG2E * math.sqrt(head.shape[0]) * norm
    room = jnp.maximum(room, 0.0) / (1.02 * math.sqrt(width))
    limit_ref[0] = room * room


def fold_weights(mask, head_w, rq, rkv, cq, ckv):
    width = rq.shape[0]
    vmem = pl.BlockSpec(memory_space=pltpu.VMEM)
    return pl.pallas_call(
        fold_kernel,
        name="fold_weights",
        out_specs=[vmem, vmem, pl.BlockSpec(memory_space=pltpu.SMEM)],
        out_shape=[jax.ShapeDtypeStruct((width, HEADS * width), BF16)] * 2
        + [jax.ShapeDtypeStruct((1,), F32)],
        cost_estimate=cost(3),
    )(mask, head_w, rq, rkv, cq, ckv)


def fetch_seq(x, dy, dz, dc):
    pairs = [
        (((y + dy) % 4) * 4 + ((z + dz) % 2) * 2 + (c + dc) % 2, y * 4 + z * 2 + c)
        for y in range(4)
        for z in range(2)
        for c in range(2)
    ]
    return lax.ppermute(x, "seq", pairs)


def fetch_row(x, dz, dx):
    pairs = [
        (((z + dz) % 2) * 4 + (i + dx) % 4, z * 4 + i) for z in range(2) for i in range(4)
    ]
    return lax.ppermute(x, "res", pairs)


def pack_kernel(*refs):
    for i, ref in enumerate(refs[:-1]):
        refs[-1][i] = ref[...]


def pack_blocks(blocks):
    first, *others = blocks[0].shape
    step = first // 4
    return pl.pallas_call(
        pack_kernel,
        grid=(4,),
        name="pack_blocks",
        in_specs=[pl.BlockSpec((step, *others), lambda i: (i, 0, 0))] * len(blocks),
        out_specs=pl.BlockSpec((len(blocks), step, *others), lambda i: (0, i, 0, 0)),
        out_shape=jax.ShapeDtypeStruct((len(blocks), first, *others), blocks[0].dtype),
        cost_estimate=cost(2),
    )(*blocks)


def hold_kernel(*refs):
    pass


def hold(*trees, micros=1):
    boxes = [dict(zip(range(len(t)), t.values())) if isinstance(t, dict) else t for t in trees]
    flat, tree = jax.tree.flatten(boxes)
    any_ = pl.BlockSpec(memory_space=pl.ANY)
    out = pl.pallas_call(
        hold_kernel,
        name="step_done",
        in_specs=[any_] * len(flat),
        out_specs=[any_] * len(flat),
        out_shape=[jax.ShapeDtypeStruct(x.shape, x.dtype) for x in flat],
        input_output_aliases={i: i for i in range(len(flat))},
        cost_estimate=cost(micros),
    )(*flat)
    out = jax.tree.unflatten(tree, out)
    return [dict(zip(t, o.values())) if isinstance(t, dict) else o for t, o in zip(trees, out)]


def per_device(
    homolog_embedding,
    pair_features,
    sequence_key_mask,
    residue_key_mask,
    pair_head_bias_matrix,
    horizontal_probe_weights,
    horizontal_lookup_weights,
    horizontal_sigmoid_weights,
    horizontal_merge_weights,
    column_query_matrix,
    vertical_lookup_weights,
    vertical_sigmoid_weights,
    vertical_merge_weights,
):
    seqs, res, width = homolog_embedding.shape
    groups = lax.axis_size("seq")
    wqk, cqk, limit = fold_weights(
        residue_key_mask.reshape(16, -1),
        pair_head_bias_matrix,
        horizontal_probe_weights,
        horizontal_lookup_weights,
        column_query_matrix,
        vertical_lookup_weights,
    )
    lookup = horizontal_lookup_weights
    a, c = {}, {}
    a[0, 0] = norm_rows(homolog_embedding, 0, seqs)
    a[0, 1] = fetch_row(a[0, 0], 0, 1)
    a[0, 3] = fetch_row(a[0, 0], 0, 3)
    a[1, 0] = fetch_row(a[0, 0], 1, 0)
    c[0, 0] = pair_bias(
        pair_features, 0, res, pair_head_bias_matrix, residue_key_mask, (a[0, 0],)
    )
    c[1, 0] = fetch_seq(c[0, 0], 1, 0, 0)
    c[3, 0] = fetch_seq(c[0, 0], 3, 0, 0)
    bias = {}

    def swap(*offsets):
        both = c[offsets[0]][None] if len(offsets) == 1 else pack_blocks([c[o] for o in offsets])
        bias[tuple((*o, 0) for o in offsets)] = both
        bias[tuple((*o, 1) for o in offsets)] = fetch_seq(both, 0, 0, 1)

    (a,) = hold(a, micros=15)
    a[1, 1] = fetch_row(a[1, 0], 0, 1)
    c[0, 1] = fetch_seq(c[0, 0], 0, 1, 0)
    a[0, 2] = fetch_row(a[0, 3], 0, 3)
    c[2, 0] = fetch_seq(c[1, 0], 1, 0, 0)
    order = ((0, 0), (0, 1), (0, 3), (1, 0), (1, 1), (0, 2), (1, 3), (1, 2))
    early = row_values([a[o] for o in order[:4]], lookup)
    queries = row_queries(a[0, 0], wqk, horizontal_sigmoid_weights, limit)
    a, early, queries, c = hold(a, early, queries, c, micros=15)
    a[1, 2] = fetch_row(a[1, 1], 0, 1)
    a[1, 3] = fetch_row(a[1, 0], 0, 3)
    c[1, 1] = fetch_seq(c[0, 1], 1, 0, 0)
    c[3, 1] = fetch_seq(c[0, 1], 3, 0, 0)
    c[2, 1] = fetch_seq(c[2, 0], 0, 1, 0)
    middle = row_values([a[o] for o in order[4:6]], lookup)
    swap(*c)
    a, middle = hold(a, middle, micros=40)
    keys = {o: a[o] for o in order}
    rest = ([*early, *middle], bias, *queries, homolog_embedding, lookup)
    rest += (horizontal_merge_weights,)
    after_rows, send = row_attention(keys, *rest)
    result = column_attention(
        lax.all_to_all(send, "seq", 0, 0, tiled=True),
        sequence_key_mask,
        cqk,
        vertical_lookup_weights,
        vertical_sigmoid_weights,
        vertical_merge_weights,
    )
    back = lax.all_to_all(result, "seq", 0, 0, tiled=True)
    return after_rows, jnp.transpose(back, (1, 0, 2, 3)).reshape(seqs, res, width)


def solution(mesh):
    return jax.shard_map(
        per_device,
        mesh=mesh,
        in_specs=(P("seq", "res", None), P("res", "seq", None)) + (P(),) * 11,
        out_specs=(P("seq", "res", None), P("seq", "res", None)),
        check_vma=False,
    )
```
